32 devices in a mesh: groups: 2 (over y), resp: 8 (over z, x), mp: 2 (over core).
Axes of the slice: x: 2, y: 2, z: 4, core: 2. Of those that a mesh axis runs over, the one named last changes fastest.
Arguments:
- query: bfloat16 [2048, 4096], P(('groups', 'resp'), 'mp'), parts along dimension 0, may hold values from -8 to 8
- saved_out: bfloat16 [2048, 4096], P(('groups', 'resp'), 'mp'), parts along dimension 0, may hold values from -6 to 6
- d_out: bfloat16 [2048, 4096], P(('groups', 'resp'), 'mp'), parts along dimension 0, may hold values from -48 to 48
- resp_kv: bfloat16 [2, 2048, 512], P(None, ('groups', 'resp'), 'mp'), parts along dimension 1, may hold values from -6 to 6
- prompt_kv: bfloat16 [2, 2048, 512], P(None, ('groups', 'resp'), 'mp'), parts along dimension 1, may hold values from -8 to 8
- prefix_blocks: int32 [16], P(('groups', 'resp')), parts along dimension 0, may hold values from 1 to 8, as said below
- resp_len: int32 [16], P(('groups', 'resp')), parts along dimension 0, may hold values from 1 to 128, as said below
- block_position: int32 [16], P(('groups', 'resp')), parts along dimension 0, may hold values from 0 to 7, as said below
Outputs:
- d_query: bfloat16 [2048, 4096], P(('groups', 'resp'), 'mp'), parts along dimension 0
- d_resp_kv: bfloat16 [2, 2048, 512], P(None, ('groups', 'resp'), 'mp'), parts along dimension 1
- d_prompt_kv: bfloat16 [2, 2048, 512], P(None, ('groups', 'resp'), 'mp'), parts along dimension 1
The draws below stay inside these ranges and needn't reach their ends.
There are 2 independent parts, one for each index of `groups`. The reference program is written for one: setup_inputs(seed, part) draws one part's arguments, and reference() takes and returns one part's arrays. A program takes and returns all parts, laid end to end along the dimension named above; each array names one. Nothing has to cross between parts.
Inputs may be any that keep to these rules, and one draw needn't show every extreme that they name: `prefix_blocks`: some response sees all 8 blocks of its prompt. `resp_len`: some response has all 128 tokens live. `block_position`: for each prompt c, the entries c, c + 1, c + 2, ... hold every position 0 to 7 once.
All inputs are finite; a program needn't handle non-finite values.
Results may differ from the reference program's by a relative error of at most 0.0051.
Values may be sent and summed in bfloat16 or wider, within the bound.
A program may use at most 64 MiB of HBM per device.

```python
import jax
import jax.numpy as jnp
from jax import lax

QH = 32
KVH = 4
HD = 128
R = 128
BLOCK = 128
G = 8
RESPS = 8
PROMPTS = 1
POOL = 1024


def draw_query(key, part):
    key = jax.random.fold_in(key, 11)
    first = jax.random.fold_in(key, 0)
    row_total = RESPS * R
    values = jnp.clip(jax.random.normal(first, (row_total, QH * HD), jnp.float32), -4.0, 4.0)
    return values.astype(jnp.bfloat16)


def draw_prompt_kv(key, part):
    key = jax.random.fold_in(key, 12)
    first = jax.random.fold_in(key, 0)
    values = jnp.clip(jax.random.normal(first, (2, POOL, KVH * HD), jnp.float32), -4.0, 4.0)
    return values.astype(jnp.bfloat16)


def draw_prefix_blocks(key, part):
    key = jax.random.fold_in(key, 13)
    first, second = jax.random.split(key)
    counts = jax.random.randint(first, (RESPS,), 1, G + 1)
    chosen = jax.random.randint(second, (), 0, RESPS)
    return counts.at[chosen].set(G).astype(jnp.int32)


def draw_resp_len(key, part):
    key = jax.random.fold_in(key, 14)
    first, second = jax.random.split(key)
    lengths = jax.random.randint(first, (RESPS,), 1, R + 1)
    chosen = jax.random.randint(second, (), 0, RESPS)
    return lengths.at[chosen].set(R).astype(jnp.int32)


def draw_block_position(key, part):
    key = jax.random.fold_in(key, 15)
    prompt_keys = jax.random.split(key, PROMPTS)
    orders = jax.vmap(lambda single: jax.random.permutation(single, G))(prompt_keys)
    return jnp.transpose(orders).reshape(RESPS).astype(jnp.int32)


def block_levels(stream_key, shape, cuts, smallest, high):
    def one(dim, shards_of):
        draws = jax.random.uniform(jax.random.fold_in(jax.random.fold_in(stream_key, 6), dim), (shards_of,), jnp.float32, smallest / len(cuts), high / len(cuts))
        return jnp.repeat(jnp.exp(draws), shape[dim] // shards_of).reshape((-1,) + (1,) * (len(shape) - dim - 1))

    loudness = one(*cuts[0])
    for cut in cuts[1:]:
        loudness = loudness * one(*cut)
    return loudness


def scatter_about(key, extent, scale, limit, pieces=(), held_as=jnp.bfloat16):
    gain = block_levels(key, extent, pieces, -0.22, 0.18) if pieces else 1.0
    values = jax.random.normal(key, extent, jnp.float32) * scale * gain
    return jnp.minimum(jnp.maximum(values, -limit), limit).astype(held_as)


def setup_inputs(seed: int = 0, part: int = 0) -> dict:
    splits = jax.random.split(jax.random.key(seed), 9)
    own_keys = jax.random.split(jax.random.fold_in(splits[8], part), 9)
    query = draw_query(jax.random.fold_in(jax.random.fold_in(splits[8], part), 71), part)
    saved_out = scatter_about(own_keys[1], (RESPS * R, QH * HD), 1.0, 6.0, ((0, 8), (1, 2)))
    d_out = scatter_about(own_keys[2], (RESPS * R, QH * HD), 8.0, 48.0, ((0, 8), (1, 2)))
    resp_kv = scatter_about(own_keys[3], (2, RESPS * R, KVH * HD), 1.0, 6.0, ((1, 8), (2, 2)))
    prompt_kv = draw_prompt_kv(jax.random.fold_in(jax.random.fold_in(splits[8], part), 71), part)
    prefix_blocks = draw_prefix_blocks(jax.random.fold_in(jax.random.fold_in(splits[8], part), 71), part)
    resp_len = draw_resp_len(jax.random.fold_in(jax.random.fold_in(splits[8], part), 71), part)
    block_position = draw_block_position(jax.random.fold_in(jax.random.fold_in(splits[8], part), 71), part)
    return {"query": query, "saved_out": saved_out, "d_out": d_out, "resp_kv": resp_kv, "prompt_kv": prompt_kv, "prefix_blocks": prefix_blocks, "resp_len": resp_len, "block_position": block_position}


blocked_score = -1.0e30


def reference(query, saved_out, d_out, resp_kv, prompt_kv, prefix_blocks, resp_len, block_position):
    ratio = QH // KVH
    span = G * BLOCK
    width = KVH * HD
    score_scale = HD ** -0.5
    row_index = jnp.arange(R, dtype=jnp.int32)
    causal = row_index[:, None] >= row_index[None, :]
    pool_view = prompt_kv.reshape(2, G, PROMPTS, BLOCK, width)
    position_view = block_position.reshape(G, PROMPTS)

    def one_response(pool_grad, response):
        prompt_id = (response % PROMPTS).astype(jnp.int32)
        start = (response * R).astype(jnp.int32)
        queries = lax.dynamic_slice_in_dim(query, start, R, 0).astype(jnp.float32).reshape(R, KVH, ratio, HD)
        outputs = lax.dynamic_slice_in_dim(saved_out, start, R, 0).astype(jnp.float32).reshape(R, KVH, ratio, HD)
        grads = lax.dynamic_slice_in_dim(d_out, start, R, 0)
        alive = row_index < resp_len[response]
        grads = jnp.where(alive[:, None], grads, jnp.zeros_like(grads)).astype(jnp.float32).reshape(R, KVH, ratio, HD)
        own_kv = lax.dynamic_slice_in_dim(resp_kv, start, R, 1)
        prompt_part = lax.dynamic_index_in_dim(pool_view, prompt_id, 2, keepdims=False).reshape(2, span, width)
        both = jnp.concatenate([prompt_part, own_kv], axis=1).astype(jnp.float32).reshape(2, span + R, KVH, HD)
        positions = lax.dynamic_index_in_dim(position_view, prompt_id, 1, keepdims=False)
        visible = jnp.repeat(positions < prefix_blocks[response], BLOCK)
        allowed = jnp.concatenate([jnp.broadcast_to(visible[None, :], (R, span)), causal], axis=1)
        scores = jnp.einsum('rgjd,tgd->gjrt', queries, both[0]) * score_scale
        scores = jnp.where(allowed, scores, blocked_score)
        row_peak = jnp.max(scores, axis=-1, keepdims=True)
        log_total = row_peak + jnp.log(jnp.sum(jnp.exp(scores - row_peak), axis=-1, keepdims=True))
        weights = jnp.exp(scores - log_total)
        weights_low = lax.optimization_barrier(weights.astype(jnp.bfloat16)).astype(jnp.float32)
        delta = jnp.transpose(jnp.sum(grads * outputs, axis=-1), (1, 2, 0))
        value_grad = jnp.einsum('gjrt,rgjd->tgd', weights_low, grads)
        weight_grad = jnp.einsum('rgjd,tgd->gjrt', grads, both[1])
        score_grad = weights * (weight_grad - delta[..., None]) * score_scale
        score_grad = lax.optimization_barrier(score_grad.astype(jnp.bfloat16)).astype(jnp.float32)
        query_grad = jnp.einsum('gjrt,tgd->rgjd', score_grad, both[0])
        key_grad = jnp.einsum('gjrt,rgjd->tgd', score_grad, queries)
        kv_grad = jnp.stack([key_grad, value_grad]).reshape(2, span + R, width)
        current = lax.dynamic_index_in_dim(pool_grad, prompt_id, 2, keepdims=False)
        updated = current + kv_grad[:, :span].reshape(2, G, BLOCK, width)
        pool_grad = lax.dynamic_update_index_in_dim(pool_grad, updated, prompt_id, 2)
        return pool_grad, (query_grad.reshape(R, QH * HD).astype(jnp.bfloat16), kv_grad[:, span:].astype(jnp.bfloat16))

    start_grad = jnp.zeros((2, G, PROMPTS, BLOCK, width), jnp.float32)
    pool_grad, (query_grads, own_grads) = lax.scan(one_response, start_grad, jnp.arange(RESPS, dtype=jnp.int32))
    d_query = query_grads.reshape(RESPS * R, QH * HD)
    d_resp_kv = jnp.transpose(own_grads, (1, 0, 2, 3)).reshape(2, RESPS * R, width)
    return d_query, d_resp_kv, pool_grad.reshape(2, POOL, width).astype(jnp.bfloat16)
```

```python
import functools
import math

import jax
import jax.numpy as jnp
from jax import lax
from jax.experimental import pallas as pl
from jax.experimental.pallas import tpu as pltpu
from jax.sharding import PartitionSpec as P

HD = 128
POS_ROWS = 16
COLS = 256
BLOCKED = -1e30
NT = (((1,), (1,)), ((), ()))


def dot(a, b):
    return jnp.dot(a, b, preferred_element_type=jnp.float32)


def dot_nt(a, b):
    return lax.dot_general(a, b, NT, preferred_element_type=jnp.float32)


def kernel(
    n, stride, kv_heads, ratio, rows,
    q_hbm, o_hbm, do_hbm, rkv_hbm, pkv_hbm, prefix_ref, len_ref, pos_ref,
    dq_ref, drkv_ref, dpkv_ref,
    q_in, o_in, do_in, q_all, do_all, kbuf, vbuf, k_t, delta, top, total,
    st, pb, ds, part, snd, rcv,
    in_sem, kv_sem, ag_send, ag_recv, rs_send, rs_recv,
):
    half = n // 2
    wide = ratio * rows
    chunks = wide // COLS
    scale = HD ** (-0.5)
    fold = scale * math.log2(math.e)

    order = {half: 2 * half}
    for step in range(2, half + 1):
        order[half + step - 1] = 2 * (step - 2)
        order[half - step + 1] = 2 * (step - 2) + 1
    order[0] = 2 * (half - 1)
    order[n] = 2 * (half - 1) + 1

    index = lax.axis_index("resp")
    me = index // stride
    lane = index % stride
    if stride == 1:
        x = me % 2
        z = me // 2
        last = (z + 1) // half
        first = (half - z) // half
        right = me + (1 - x) * (2 - last) + x * (first - 2)
        left = me + (1 - x) * (3 * first - 2) + x * (2 - 3 * last)
    else:
        right = (me + 1) % n
        left = (me + n - 1) % n
    right = right * stride + lane
    left = left * stride + lane

    kv_copies = []
    for g in range(kv_heads):
        cols = pl.ds(g * HD, HD)
        kv_copies.append(pltpu.make_async_copy(
            pkv_hbm.at[0, :, cols], kbuf.at[g, order[0], pl.ds(0, rows)], kv_sem.at[0, g]))
        kv_copies.append(pltpu.make_async_copy(
            pkv_hbm.at[1, :, cols], vbuf.at[g, order[0]], kv_sem.at[1, g]))
        kv_copies.append(pltpu.make_async_copy(
            rkv_hbm.at[0, :, cols], kbuf.at[g, order[n], pl.ds(0, rows)], kv_sem.at[2, g]))
        kv_copies.append(pltpu.make_async_copy(
            rkv_hbm.at[1, :, cols], vbuf.at[g, order[n]], kv_sem.at[3, g]))
    in_copies = [
        pltpu.make_async_copy(q_hbm, q_in, in_sem.at[0]),
        pltpu.make_async_copy(do_hbm, do_in, in_sem.at[1]),
        pltpu.make_async_copy(o_hbm, o_in, in_sem.at[2]),
    ]
    for copy in kv_copies + in_copies:
        copy.start()

    barrier = pltpu.get_barrier_semaphore()
    for near in (left, right):
        pl.semaphore_signal(
            barrier, inc=1, device_id={"resp": near}, device_id_type=pl.DeviceIdType.MESH)
    position = jnp.full((POS_ROWS, HD), pos_ref[0], jnp.int32).astype(jnp.float32)
    for g in range(kv_heads):
        kbuf[g, order[0], rows:rows + POS_ROWS, :] = position.astype(jnp.bfloat16)
    pl.semaphore_wait(barrier, 2)
    for copy in kv_copies:
        copy.wait()

    def send(src, dst, send_sem, recv_sem, way):
        return pltpu.make_async_remote_copy(
            src_ref=src, dst_ref=dst, send_sem=send_sem, recv_sem=recv_sem,
            device_id={"resp": right if way == 0 else left},
            device_id_type=pl.DeviceIdType.MESH)

    def gather_copy(kind, way, step):
        buf = kbuf if kind == 0 else vbuf
        if way == 0:
            source, target = order[step - 1], order[step]
        else:
            source, target = order[(n - step + 1) % n], order[n - step]
        if step == half:
            src, dst = buf.at[way, source], buf.at[way, target]
        else:
            src, dst = buf.at[:, source], buf.at[:, target]
        return send(src, dst, ag_send.at[kind, way, step - 1], ag_recv.at[kind, way, step - 1], way)

    gather = {
        (kind, way, step): gather_copy(kind, way, step)
        for kind in range(2) for way in range(2) for step in range(1, half + 1)
    }

    def start_gather(kind, step):
        for way in range(2):
            gather[kind, way, step].start()

    def wait_gather(kind, step):
        for way in range(2):
            gather[kind, way, step].wait_recv()

    start_gather(0, 1)
    start_gather(1, 1)

    for copy in in_copies:
        copy.wait()
    live = lax.broadcasted_iota(jnp.int32, (rows, HD), 0) < len_ref[0]
    for g in range(kv_heads):
        for j in range(ratio):
            cols = slice((g * ratio + j) * HD, (g * ratio + j + 1) * HD)
            place = slice(j * rows, (j + 1) * rows)
            q_all[g, place, :] = q_in[:, cols]
            grads = jnp.where(live, do_in[:, cols].astype(jnp.float32), 0.0)
            do_all[g, place, :] = grads.astype(jnp.bfloat16)
            product = jnp.transpose(grads * o_in[:, cols].astype(jnp.float32))
            delta[g, :, place] = jnp.sum(product, axis=0, keepdims=True)

    def forward(slot, start=False):
        spot = order[slot]
        if slot == n:
            allowed = None
        else:
            seen = kbuf[0, spot, rows:rows + 8, :].astype(jnp.float32)[0:1, :]
            bias = jnp.where(seen < prefix_ref[0].astype(jnp.float32), 0.0, BLOCKED)
            bias = jnp.concatenate([bias] * (COLS // HD), axis=1)

        def head(g, carry):
            keys = kbuf[g, spot, 0:rows, :]
            k_t[g, :, spot * rows:(spot + 1) * rows] = jnp.transpose(
                keys.astype(jnp.float32)).astype(jnp.bfloat16)
            for c in range(chunks):
                cols = slice(c * COLS, (c + 1) * COLS)
                scores = dot_nt(keys, q_all[g, cols, :]) * fold
                if slot == n:
                    key_index = lax.broadcasted_iota(jnp.int32, (rows, COLS), 0)
                    row_index = lax.broadcasted_iota(jnp.int32, (rows, COLS), 1) % rows
                    scores = jnp.where(key_index <= row_index, scores, BLOCKED)
                else:
                    scores = scores + bias
                st[g, spot * rows:(spot + 1) * rows, cols] = scores
                peak = jnp.max(scores, axis=0, keepdims=True)
                if start:
                    top[g, :, cols] = peak
                    total[g, :, cols] = jnp.sum(jnp.exp2(scores - peak), axis=0, keepdims=True)
                else:
                    old = top[g, :, cols]
                    new = jnp.maximum(old, peak)
                    top[g, :, cols] = new
                    total[g, :, cols] = total[g, :, cols] * jnp.exp2(old - new) + jnp.sum(
                        jnp.exp2(scores - new), axis=0, keepdims=True)
            return carry

        lax.fori_loop(0, kv_heads, head, 0)

    forward(n, True)
    forward(0)
    for step in range(1, half + 1):
        wait_gather(0, step)
        if step < half:
            start_gather(0, step + 1)
        if step > 1:
            wait_gather(1, step - 1)
            start_gather(1, step)
        forward(step)
        if step < half:
            forward(n - step)

    for g in range(kv_heads):
        top[g] = top[g] + jnp.log2(total[g])

    def value_side(spot, count):
        def head(g, carry):
            for b in range(count):
                span = slice((spot + b) * rows, (spot + b + 1) * rows)
                for c in range(chunks):
                    cols = slice(c * COLS, (c + 1) * COLS)
                    weights = jnp.exp2(st[g, span, cols] - top[g, :, cols])
                    st[g, span, cols] = weights
                    pb[b * rows:(b + 1) * rows, cols] = weights.astype(jnp.bfloat16)
            part[1, g, spot * rows:(spot + count) * rows, :] = dot(
                pb[0:count * rows, :], do_all[g])
            return carry

        lax.fori_loop(0, kv_heads, head, 0)

    def key_side(spot, count):
        def head(g, carry):
            for b in range(count):
                span = slice((spot + b) * rows, (spot + b + 1) * rows)
                values = vbuf[g, spot + b]
                for c in range(chunks):
                    cols = slice(c * COLS, (c + 1) * COLS)
                    moved = dot_nt(values, do_all[g, cols, :])
                    ds[g, span, cols] = (
                        st[g, span, cols] * (moved - delta[g, :, cols]) * scale
                    ).astype(jnp.bfloat16)
            part[0, g, spot * rows:(spot + count) * rows, :] = dot(
                ds[g, spot * rows:(spot + count) * rows, :], q_all[g])
            return carry

        lax.fori_loop(0, kv_heads, head, 0)

    def own(kind, g, spot):
        return part[kind, g, spot * rows:(spot + 1) * rows, :]

    def back_copy(kind, way, step):
        src, dst = snd.at[kind, way, step - 1], rcv.at[kind, way, step - 1]
        if step == 1:
            src, dst = src.at[way], dst.at[way]
        return send(src, dst, rs_send.at[kind, way, step - 1], rs_recv.at[kind, way, step - 1], way)

    back = {
        (kind, way, step): back_copy(kind, way, step)
        for kind in range(2) for way in range(2) for step in range(1, half + 1)
    }

    value_side(order[half], 1)
    for way in range(2):
        snd[1, way, 0, way] = own(1, way, order[half]).astype(jnp.bfloat16)
        back[1, way, 1].start()
    wait_gather(1, half)
    key_side(order[half], 1)
    for way in range(2):
        snd[0, way, 0, way] = own(0, way, order[half]).astype(jnp.bfloat16)
        back[0, way, 1].start()

    for step in range(2, half + 1):
        spot = 2 * (step - 2)
        value_side(spot, 2)
        key_side(spot, 2)
        for kind in (1, 0):
            for way in range(2):
                back[kind, way, step - 1].wait_recv()
                for g in range(kv_heads):
                    mine = own(kind, g, spot + way)
                    if step > 2 or g == way:
                        mine = mine + rcv[kind, way, step - 2, g].astype(jnp.float32)
                    snd[kind, way, step - 1, g] = mine.astype(jnp.bfloat16)
                back[kind, way, step].start()

    spot = 2 * (half - 1)
    value_side(spot, 2)
    key_side(spot, 2)
    for kind in range(2):
        for g in range(kv_heads):
            drkv_ref[kind, :, g * HD:(g + 1) * HD] = own(kind, g, spot + 1).astype(jnp.bfloat16)
    for g in range(kv_heads):
        for c in range(chunks):
            turned = dot(k_t[g], ds[g, :, c * COLS:(c + 1) * COLS])
            for j in range(COLS // rows):
                column = (g * ratio + c * (COLS // rows) + j) * HD
                dq_ref[:, column:column + HD] = jnp.transpose(
                    turned[:, j * rows:(j + 1) * rows]).astype(jnp.bfloat16)
    for kind in (1, 0):
        for way in range(2):
            back[kind, way, half].wait_recv()
        for g in range(kv_heads):
            summed = own(kind, g, spot)
            for way in range(2):
                summed = summed + rcv[kind, way, half - 1, g].astype(jnp.float32)
            dpkv_ref[kind, :, g * HD:(g + 1) * HD] = summed.astype(jnp.bfloat16)

    for copy in list(gather.values()) + list(back.values()):
        copy.wait_send()


def on_device(query, saved_out, d_out, resp_kv, prompt_kv, prefix_blocks, resp_len, block_position):
    rows = query.shape[0]
    kv_heads = resp_kv.shape[2] // HD
    ratio = query.shape[1] // HD // kv_heads
    axis_total = lax.axis_size("resp")
    n = min(16, axis_total)
    stride = axis_total // n
    half = n // 2
    wide = ratio * rows
    keys = (n + 1) * rows
    low, full = jnp.bfloat16, jnp.float32
    anywhere = pl.BlockSpec(memory_space=pl.ANY)
    vmem = pl.BlockSpec(memory_space=pltpu.VMEM)
    smem = pl.BlockSpec(memory_space=pltpu.SMEM)
    dma = pltpu.SemaphoreType.DMA
    return pl.pallas_call(
        functools.partial(kernel, n, stride, kv_heads, ratio, rows),
        out_shape=(
            jax.ShapeDtypeStruct(query.shape, low),
            jax.ShapeDtypeStruct(resp_kv.shape, low),
            jax.ShapeDtypeStruct(prompt_kv.shape, low),
        ),
        in_specs=[anywhere] * 5 + [smem] * 3,
        out_specs=(vmem, vmem, vmem),
        scratch_shapes=[
            pltpu.VMEM(query.shape, low),
            pltpu.VMEM(query.shape, low),
            pltpu.VMEM(query.shape, low),
            pltpu.VMEM((kv_heads, wide, HD), low),
            pltpu.VMEM((kv_heads, wide, HD), low),
            pltpu.VMEM((kv_heads, n + 1, rows + POS_ROWS, HD), low),
            pltpu.VMEM((kv_heads, n + 1, rows, HD), low),
            pltpu.VMEM((kv_heads, HD, keys), low),
            pltpu.VMEM((kv_heads, 1, wide), full),
            pltpu.VMEM((kv_heads, 1, wide), full),
            pltpu.VMEM((kv_heads, 1, wide), full),
            pltpu.VMEM((kv_heads, keys, wide), full),
            pltpu.VMEM((2 * rows, wide), low),
            pltpu.VMEM((kv_heads, keys, wide), low),
            pltpu.VMEM((2, kv_heads, keys, HD), full),
            pltpu.VMEM((2, 2, half, kv_heads, rows, HD), low),
            pltpu.VMEM((2, 2, half, kv_heads, rows, HD), low),
            dma((3,)),
            dma((4, kv_heads)),
            dma((2, 2, half)),
            dma((2, 2, half)),
            dma((2, 2, half)),
            dma((2, 2, half)),
        ],
        compiler_params=pltpu.CompilerParams(
            collective_id=0, has_side_effects=True, vmem_limit_bytes=56 * 2**20),
    )(query, saved_out, d_out, resp_kv, prompt_kv, prefix_blocks, resp_len, block_position)


def solution(mesh):
    placed = (
        P(("groups", "resp"), "mp"),
        P(("groups", "resp"), "mp"),
        P(("groups", "resp"), "mp"),
        P(None, ("groups", "resp"), "mp"),
        P(None, ("groups", "resp"), "mp"),
        P(("groups", "resp")),
        P(("groups", "resp")),
        P(("groups", "resp")),
    )
    return jax.shard_map(
        on_device,
        mesh=mesh,
        in_specs=placed,
        out_specs=(
            P(("groups", "resp"), "mp"),
            P(None, ("groups", "resp"), "mp"),
            P(None, ("groups", "resp"), "mp"),
        ),
        check_vma=False,
    )
```

```python
import functools
import math

import jax
import jax.numpy as jnp
from jax import lax
from jax.experimental import pallas as pl
from jax.experimental.pallas import tpu as pltpu
from jax.sharding import PartitionSpec as P

HD = 128
POS_ROWS = 16
COLS = 256
BLOCKED = -1e30
NT = (((1,), (1,)), ((), ()))


def dot(a, b):
    return jnp.dot(a, b, preferred_element_type=jnp.float32)


def dot_nt(a, b):
    return lax.dot_general(a, b, NT, preferred_element_type=jnp.float32)


def kernel(
    n, stride, kv_heads, ratio, rows,
    q_hbm, o_hbm, do_hbm, rkv_hbm, pkv_hbm, prefix_ref, len_ref, pos_ref,
    dq_ref, drkv_ref, dpkv_ref,
    q_in, o_in, do_in, q_all, do_all, kbuf, vbuf, k_t, delta, top, total,
    st, pb, ds, part, snd, rcv, drkv, dpkv,
    in_sem, out_sem, kv_sem, ag_send, ag_recv, rs_send, rs_recv,
):
    half = n // 2
    wide = ratio * rows
    chunks = wide // COLS
    scale = HD ** (-0.5)
    fold = scale * math.log2(math.e)

    order = {half: 2 * half}
    for step in range(2, half + 1):
        order[half + step - 1] = 2 * (step - 2)
        order[half - step + 1] = 2 * (step - 2) + 1
    order[0] = 2 * (half - 1)
    order[n] = 2 * (half - 1) + 1

    index = lax.axis_index("resp")
    me = index // stride
    lane = index % stride
    if stride == 1:
        x = me % 2
        z = me // 2
        last = (z + 1) // half
        first = (half - z) // half
        right = me + (1 - x) * (2 - last) + x * (first - 2)
        left = me + (1 - x) * (3 * first - 2) + x * (2 - 3 * last)
    else:
        right = (me + 1) % n
        left = (me + n - 1) % n
    right = right * stride + lane
    left = left * stride + lane

    kv_copies = []
    for g in range(kv_heads):
        cols = pl.ds(g * HD, HD)
        kv_copies.append(pltpu.make_async_copy(
            pkv_hbm.at[0, :, cols], kbuf.at[g, order[0], pl.ds(0, rows)], kv_sem.at[0, g]))
        kv_copies.append(pltpu.make_async_copy(
            pkv_hbm.at[1, :, cols], vbuf.at[g, order[0]], kv_sem.at[1, g]))
        kv_copies.append(pltpu.make_async_copy(
            rkv_hbm.at[0, :, cols], kbuf.at[g, order[n], pl.ds(0, rows)], kv_sem.at[2, g]))
        kv_copies.append(pltpu.make_async_copy(
            rkv_hbm.at[1, :, cols], vbuf.at[g, order[n]], kv_sem.at[3, g]))
    in_copies = [
        pltpu.make_async_copy(q_hbm, q_in, in_sem.at[0]),
        pltpu.make_async_copy(do_hbm, do_in, in_sem.at[1]),
        pltpu.make_async_copy(o_hbm, o_in, in_sem.at[2]),
    ]
    for copy in kv_copies + in_copies:
        copy.start()

    barrier = pltpu.get_barrier_semaphore()
    for near in (left, right):
        pl.semaphore_signal(
            barrier, inc=1, device_id={"resp": near}, device_id_type=pl.DeviceIdType.MESH)
    position = jnp.full((POS_ROWS, HD), pos_ref[0], jnp.int32).astype(jnp.float32)
    for g in range(kv_heads):
        kbuf[g, order[0], rows:rows + POS_ROWS, :] = position.astype(jnp.bfloat16)
    pl.semaphore_wait(barrier, 2)
    for copy in kv_copies:
        copy.wait()

    def send(src, dst, send_sem, recv_sem, way):
        return pltpu.make_async_remote_copy(
            src_ref=src, dst_ref=dst, send_sem=send_sem, recv_sem=recv_sem,
            device_id={"resp": right if way == 0 else left},
            device_id_type=pl.DeviceIdType.MESH)

    def gather_copy(kind, way, step, g):
        buf = kbuf if kind == 0 else vbuf
        if way == 0:
            source, target = order[step - 1], order[step]
        else:
            source, target = order[(n - step + 1) % n], order[n - step]
        return send(
            buf.at[g, source], buf.at[g, target],
            ag_send.at[kind, way, step - 1, g], ag_recv.at[kind, way, step - 1, g], way)

    def carried(way, step, g):
        return step < half or g == way

    gather = {
        (kind, way, step, g): gather_copy(kind, way, step, g)
        for kind in range(2) for way in range(2) for step in range(1, half + 1)
        for g in range(kv_heads) if carried(way, step, g)
    }

    def pass_on(kind, step):
        for g in range(kv_heads):
            for way in range(2):
                if step > 0 and (kind, way, step, g) in gather:
                    gather[kind, way, step, g].wait_recv()
                if (kind, way, step + 1, g) in gather:
                    gather[kind, way, step + 1, g].start()

    pass_on(0, 0)
    pass_on(1, 0)

    for copy in in_copies:
        copy.wait()
    live = lax.broadcasted_iota(jnp.int32, (rows, HD), 0) < len_ref[0]
    for g in range(kv_heads):
        for j in range(ratio):
            cols = slice((g * ratio + j) * HD, (g * ratio + j + 1) * HD)
            place = slice(j * rows, (j + 1) * rows)
            q_all[g, place, :] = q_in[:, cols]
            grads = jnp.where(live, do_in[:, cols].astype(jnp.float32), 0.0)
            do_all[g, place, :] = grads.astype(jnp.bfloat16)
            product = jnp.transpose(grads * o_in[:, cols].astype(jnp.float32))
            delta[g, :, place] = jnp.sum(product, axis=0, keepdims=True)

    def forward(slot, start=False):
        spot = order[slot]
        if slot == n:
            allowed = None
        else:
            seen = kbuf[0, spot, rows:rows + 8, :].astype(jnp.float32)[0:1, :]
            bias = jnp.where(seen < prefix_ref[0].astype(jnp.float32), 0.0, BLOCKED)
            bias = jnp.concatenate([bias] * (COLS // HD), axis=1)

        def head(g, carry):
            keys = kbuf[g, spot, 0:rows, :]
            k_t[g, :, spot * rows:(spot + 1) * rows] = jnp.transpose(
                keys.astype(jnp.float32)).astype(jnp.bfloat16)
            for c in range(chunks):
                cols = slice(c * COLS, (c + 1) * COLS)
                scores = dot_nt(keys, q_all[g, cols, :]) * fold
                if slot == n:
                    key_index = lax.broadcasted_iota(jnp.int32, (rows, COLS), 0)
                    row_index = lax.broadcasted_iota(jnp.int32, (rows, COLS), 1) % rows
                    scores = jnp.where(key_index <= row_index, scores, BLOCKED)
                else:
                    scores = scores + bias
                st[g, spot * rows:(spot + 1) * rows, cols] = scores
                peak = jnp.max(scores, axis=0, keepdims=True)
                if start:
                    top[g, :, cols] = peak
                    total[g, :, cols] = jnp.sum(jnp.exp2(scores - peak), axis=0, keepdims=True)
                else:
                    old = top[g, :, cols]
                    new = jnp.maximum(old, peak)
                    top[g, :, cols] = new
                    total[g, :, cols] = total[g, :, cols] * jnp.exp2(old - new) + jnp.sum(
                        jnp.exp2(scores - new), axis=0, keepdims=True)
            return carry

        lax.fori_loop(0, kv_heads, head, 0)

    forward(n, True)
    forward(0)
    for step in range(1, half + 1):
        pass_on(0, step)
        if step < half:
            pass_on(1, step)
        forward(step)
        if step < half:
            forward(n - step)

    for g in range(kv_heads):
        top[g] = top[g] + jnp.log2(total[g])

    def value_side(spot, count):
        def head(g, carry):
            for b in range(count):
                span = slice((spot + b) * rows, (spot + b + 1) * rows)
                for c in range(chunks):
                    cols = slice(c * COLS, (c + 1) * COLS)
                    weights = jnp.exp2(st[g, span, cols] - top[g, :, cols])
                    st[g, span, cols] = weights
                    pb[b * rows:(b + 1) * rows, cols] = weights.astype(jnp.bfloat16)
            part[1, g, spot * rows:(spot + count) * rows, :] = dot(
                pb[0:count * rows, :], do_all[g])
            return carry

        lax.fori_loop(0, kv_heads, head, 0)

    def key_side(spot, count):
        def head(g, carry):
            for b in range(count):
                span = slice((spot + b) * rows, (spot + b + 1) * rows)
                values = vbuf[g, spot + b]
                for c in range(chunks):
                    cols = slice(c * COLS, (c + 1) * COLS)
                    moved = dot_nt(values, do_all[g, cols, :])
                    ds[g, span, cols] = (
                        st[g, span, cols] * (moved - delta[g, :, cols]) * scale
                    ).astype(jnp.bfloat16)
            part[0, g, spot * rows:(spot + count) * rows, :] = dot(
                ds[g, spot * rows:(spot + count) * rows, :], q_all[g])
            return carry

        lax.fori_loop(0, kv_heads, head, 0)

    def own(kind, g, spot):
        return part[kind, g, spot * rows:(spot + 1) * rows, :]

    def back_copy(kind, way, step, g):
        return send(
            snd.at[kind, way, step - 1, g], rcv.at[kind, way, step - 1, g],
            rs_send.at[kind, way, step - 1, g], rs_recv.at[kind, way, step - 1, g], way)

    back = {
        (kind, way, step, g): back_copy(kind, way, step, g)
        for kind in range(2) for way in range(2) for step in range(1, half + 1)
        for g in range(kv_heads) if step > 1 or g == way
    }

    value_side(order[half], 1)
    for way in range(2):
        snd[1, way, 0, way] = own(1, way, order[half]).astype(jnp.bfloat16)
        back[1, way, 1, way].start()
    pass_on(1, half)
    key_side(order[half], 1)
    for way in range(2):
        snd[0, way, 0, way] = own(0, way, order[half]).astype(jnp.bfloat16)
        back[0, way, 1, way].start()

    for step in range(2, half + 1):
        spot = 2 * (step - 2)
        value_side(spot, 2)
        key_side(spot, 2)
        for kind in (1, 0):
            pairs = [(g, way) for g in range(kv_heads) for way in range(2)]
            if step == 2:
                pairs.sort(key=lambda pair: pair[0] == pair[1])
            for g, way in pairs:
                mine = own(kind, g, spot + way)
                if (kind, way, step - 1, g) in back:
                    back[kind, way, step - 1, g].wait_recv()
                    mine = mine + rcv[kind, way, step - 2, g].astype(jnp.float32)
                snd[kind, way, step - 1, g] = mine.astype(jnp.bfloat16)
                back[kind, way, step, g].start()

    spot = 2 * (half - 1)
    value_side(spot, 2)
    key_side(spot, 2)
    for kind in range(2):
        for g in range(kv_heads):
            drkv[kind, :, g * HD:(g + 1) * HD] = own(kind, g, spot + 1).astype(jnp.bfloat16)
    for g in range(kv_heads):
        for c in range(chunks):
            turned = dot(k_t[g], ds[g, :, c * COLS:(c + 1) * COLS])
            for j in range(COLS // rows):
                column = (g * ratio + c * (COLS // rows) + j) * HD
                q_in[:, column:column + HD] = jnp.transpose(
                    turned[:, j * rows:(j + 1) * rows]).astype(jnp.bfloat16)
    out_copies = [
        pltpu.make_async_copy(q_in, dq_ref, out_sem.at[0]),
        pltpu.make_async_copy(drkv, drkv_ref, out_sem.at[1]),
        pltpu.make_async_copy(dpkv, dpkv_ref, out_sem.at[2]),
    ]
    out_copies[0].start()
    out_copies[1].start()
    for kind in (1, 0):
        for g in range(kv_heads):
            summed = own(kind, g, spot)
            for way in range(2):
                back[kind, way, half, g].wait_recv()
                summed = summed + rcv[kind, way, half - 1, g].astype(jnp.float32)
            dpkv[kind, :, g * HD:(g + 1) * HD] = summed.astype(jnp.bfloat16)
    out_copies[2].start()

    for copy in list(gather.values()) + list(back.values()):
        copy.wait_send()
    for copy in out_copies:
        copy.wait()


def hand_out(a, b, c, a_out, b_out, c_out, a_held, b_held, c_held, in_sem, out_sem):
    triples = ((a, a_held, a_out), (b, b_held, b_out), (c, c_held, c_out))
    taken = [pltpu.make_async_copy(t[0], t[1], in_sem.at[i]) for i, t in enumerate(triples)]
    given = [pltpu.make_async_copy(t[1], t[2], out_sem.at[i]) for i, t in enumerate(triples)]
    for copy in taken:
        copy.start()
    for copy, after in zip(taken, given):
        copy.wait()
        after.start()
    for copy in given:
        copy.wait()


def on_device(query, saved_out, d_out, resp_kv, prompt_kv, prefix_blocks, resp_len, block_position):
    rows = query.shape[0]
    kv_heads = resp_kv.shape[2] // HD
    ratio = query.shape[1] // HD // kv_heads
    axis_total = lax.axis_size("resp")
    n = min(16, axis_total)
    stride = axis_total // n
    half = n // 2
    wide = ratio * rows
    keys = (n + 1) * rows
    low, full = jnp.bfloat16, jnp.float32
    anywhere = pl.BlockSpec(memory_space=pl.ANY)
    smem = pl.BlockSpec(memory_space=pltpu.SMEM)
    dma = pltpu.SemaphoreType.DMA
    results = pl.pallas_call(
        functools.partial(kernel, n, stride, kv_heads, ratio, rows),
        out_shape=(
            jax.ShapeDtypeStruct(query.shape, low),
            jax.ShapeDtypeStruct(resp_kv.shape, low),
            jax.ShapeDtypeStruct(prompt_kv.shape, low),
        ),
        in_specs=[anywhere] * 5 + [smem] * 3,
        out_specs=(anywhere, anywhere, anywhere),
        scratch_shapes=[
            pltpu.VMEM(query.shape, low),
            pltpu.VMEM(query.shape, low),
            pltpu.VMEM(query.shape, low),
            pltpu.VMEM((kv_heads, wide, HD), low),
            pltpu.VMEM((kv_heads, wide, HD), low),
            pltpu.VMEM((kv_heads, n + 1, rows + POS_ROWS, HD), low),
            pltpu.VMEM((kv_heads, n + 1, rows, HD), low),
            pltpu.VMEM((kv_heads, HD, keys), low),
            pltpu.VMEM((kv_heads, 1, wide), full),
            pltpu.VMEM((kv_heads, 1, wide), full),
            pltpu.VMEM((kv_heads, 1, wide), full),
            pltpu.VMEM((kv_heads, keys, wide), full),
            pltpu.VMEM((2 * rows, wide), low),
            pltpu.VMEM((kv_heads, keys, wide), low),
            pltpu.VMEM((2, kv_heads, keys, HD), full),
            pltpu.VMEM((2, 2, half, kv_heads, rows, HD), low),
            pltpu.VMEM((2, 2, half, kv_heads, rows, HD), low),
            pltpu.VMEM(resp_kv.shape, low),
            pltpu.VMEM(prompt_kv.shape, low),
            dma((3,)),
            dma((3,)),
            dma((4, kv_heads)),
            dma((2, 2, half, kv_heads)),
            dma((2, 2, half, kv_heads)),
            dma((2, 2, half, kv_heads)),
            dma((2, 2, half, kv_heads)),
        ],
        compiler_params=pltpu.CompilerParams(
            collective_id=0, has_side_effects=True, vmem_limit_bytes=56 * 2**20),
    )(query, saved_out, d_out, resp_kv, prompt_kv, prefix_blocks, resp_len, block_position)
    return pl.pallas_call(
        hand_out,
        out_shape=tuple(jax.ShapeDtypeStruct(r.shape, r.dtype) for r in results),
        in_specs=[anywhere] * 3,
        out_specs=(anywhere,) * 3,
        scratch_shapes=[pltpu.VMEM(r.shape, r.dtype) for r in results] + [dma((3,)), dma((3,))],
    )(*results)


def solution(mesh):
    placed = (
        P(("groups", "resp"), "mp"),
        P(("groups", "resp"), "mp"),
        P(("groups", "resp"), "mp"),
        P(None, ("groups", "resp"), "mp"),
        P(None, ("groups", "resp"), "mp"),
        P(("groups", "resp")),
        P(("groups", "resp")),
        P(("groups", "resp")),
    )
    return jax.shard_map(
        on_device,
        mesh=mesh,
        in_specs=placed,
        out_specs=(
            P(("groups", "resp"), "mp"),
            P(None, ("groups", "resp"), "mp"),
            P(None, ("groups", "resp"), "mp"),
        ),
        check_vma=False,
    )
```

```python
import functools
import math

import jax
import jax.numpy as jnp
from jax import lax
from jax.experimental import pallas as pl
from jax.experimental.pallas import tpu as pltpu
from jax.sharding import PartitionSpec as P

HD = 128
POS_ROWS = 16
COLS = 256
BLOCKED = -1e30
NT = (((1,), (1,)), ((), ()))


def dot(a, b):
    return jnp.dot(a, b, preferred_element_type=jnp.float32)


def dot_nt(a, b):
    return lax.dot_general(a, b, NT, preferred_element_type=jnp.float32)


def kernel(
    n, stride, kv_heads, ratio, rows,
    q_hbm, o_hbm, do_hbm, rkv_hbm, pkv_hbm, prefix_ref, len_ref, pos_ref,
    dq_ref, drkv_ref, dpkv_ref,
    q_in, o_in, do_in, q_all, do_all, kbuf, vbuf, k_t, delta, top, total,
    st, pb, ds, part, snd, rcv, drkv, dpkv,
    in_sem, out_sem, kv_sem, ag_send, ag_recv, rs_send, rs_recv,
):
    half = n // 2
    wide = ratio * rows
    chunks = wide // COLS
    scale = HD ** (-0.5)
    fold = scale * math.log2(math.e)

    order = {half: 2 * half}
    for step in range(2, half + 1):
        order[half + step - 1] = 2 * (step - 2)
        order[half - step + 1] = 2 * (step - 2) + 1
    order[0] = 2 * (half - 1)
    order[n] = 2 * (half - 1) + 1

    index = lax.axis_index("resp")
    me = index // stride
    lane = index % stride
    if stride == 1:
        x = me % 2
        z = me // 2
        last = (z + 1) // half
        first = (half - z) // half
        right = me + (1 - x) * (2 - last) + x * (first - 2)
        left = me + (1 - x) * (3 * first - 2) + x * (2 - 3 * last)
    else:
        right = (me + 1) % n
        left = (me + n - 1) % n
    right = right * stride + lane
    left = left * stride + lane

    kv_copies = []
    for g in range(kv_heads):
        cols = pl.ds(g * HD, HD)
        kv_copies.append(pltpu.make_async_copy(
            pkv_hbm.at[0, :, cols], kbuf.at[g, order[0], pl.ds(0, rows)], kv_sem.at[0, g]))
        kv_copies.append(pltpu.make_async_copy(
            pkv_hbm.at[1, :, cols], vbuf.at[g, order[0]], kv_sem.at[1, g]))
        kv_copies.append(pltpu.make_async_copy(
            rkv_hbm.at[0, :, cols], kbuf.at[g, order[n], pl.ds(0, rows)], kv_sem.at[2, g]))
        kv_copies.append(pltpu.make_async_copy(
            rkv_hbm.at[1, :, cols], vbuf.at[g, order[n]], kv_sem.at[3, g]))
    in_copies = [
        pltpu.make_async_copy(q_hbm, q_in, in_sem.at[0]),
        pltpu.make_async_copy(do_hbm, do_in, in_sem.at[1]),
        pltpu.make_async_copy(o_hbm, o_in, in_sem.at[2]),
    ]
    for copy in kv_copies + in_copies:
        copy.start()

    barrier = pltpu.get_barrier_semaphore()
    for near in (left, right):
        pl.semaphore_signal(
            barrier, inc=1, device_id={"resp": near}, device_id_type=pl.DeviceIdType.MESH)
    position = jnp.full((POS_ROWS, HD), pos_ref[0], jnp.int32).astype(jnp.float32)
    for g in range(kv_heads):
        kbuf[g, order[0], rows:rows + POS_ROWS, :] = position.astype(jnp.bfloat16)
    pl.semaphore_wait(barrier, 2)
    for g in range(kv_heads):
        kv_copies[4 * g].wait()
        kv_copies[4 * g + 1].wait()

    def send(src, dst, send_sem, recv_sem, way):
        return pltpu.make_async_remote_copy(
            src_ref=src, dst_ref=dst, send_sem=send_sem, recv_sem=recv_sem,
            device_id={"resp": right if way == 0 else left},
            device_id_type=pl.DeviceIdType.MESH)

    def gather_copy(kind, way, step, g):
        buf = kbuf if kind == 0 else vbuf
        if way == 0:
            source, target = order[step - 1], order[step]
        else:
            source, target = order[(n - step + 1) % n], order[n - step]
        return send(
            buf.at[g, source], buf.at[g, target],
            ag_send.at[kind, way, step - 1, g], ag_recv.at[kind, way, step - 1, g], way)

    def carried(way, step, g):
        return step < half or g == way

    gather = {
        (kind, way, step, g): gather_copy(kind, way, step, g)
        for kind in range(2) for way in range(2) for step in range(1, half + 1)
        for g in range(kv_heads) if carried(way, step, g)
    }

    def pass_on(kind, step):
        for g in range(kv_heads):
            for way in range(2):
                if step > 0 and (kind, way, step, g) in gather:
                    gather[kind, way, step, g].wait_recv()
                if (kind, way, step + 1, g) in gather:
                    gather[kind, way, step + 1, g].start()

    pass_on(0, 0)
    pass_on(1, 0)

    for g in range(kv_heads):
        kv_copies[4 * g + 2].wait()
        kv_copies[4 * g + 3].wait()
    for copy in in_copies:
        copy.wait()
    live = lax.broadcasted_iota(jnp.int32, (rows, HD), 0) < len_ref[0]
    for g in range(kv_heads):
        for j in range(ratio):
            cols = slice((g * ratio + j) * HD, (g * ratio + j + 1) * HD)
            place = slice(j * rows, (j + 1) * rows)
            q_all[g, place, :] = q_in[:, cols]
            grads = jnp.where(live, do_in[:, cols].astype(jnp.float32), 0.0)
            do_all[g, place, :] = grads.astype(jnp.bfloat16)
            product = jnp.transpose(grads * o_in[:, cols].astype(jnp.float32))
            delta[g, :, place] = jnp.sum(product, axis=0, keepdims=True)

    def forward(slot, start=False):
        spot = order[slot]
        if slot == n:
            allowed = None
        else:
            seen = kbuf[0, spot, rows:rows + 8, :].astype(jnp.float32)[0:1, :]
            bias = jnp.where(seen < prefix_ref[0].astype(jnp.float32), 0.0, BLOCKED)
            bias = jnp.concatenate([bias] * (COLS // HD), axis=1)

        def head(g, carry):
            keys = kbuf[g, spot, 0:rows, :]
            k_t[g, :, spot * rows:(spot + 1) * rows] = jnp.transpose(
                keys.astype(jnp.float32)).astype(jnp.bfloat16)
            for c in range(chunks):
                cols = slice(c * COLS, (c + 1) * COLS)
                scores = dot_nt(keys, q_all[g, cols, :]) * fold
                if slot == n:
                    key_index = lax.broadcasted_iota(jnp.int32, (rows, COLS), 0)
                    row_index = lax.broadcasted_iota(jnp.int32, (rows, COLS), 1) % rows
                    scores = jnp.where(key_index <= row_index, scores, BLOCKED)
                else:
                    scores = scores + bias
                st[g, spot * rows:(spot + 1) * rows, cols] = scores
                peak = jnp.max(scores, axis=0, keepdims=True)
                if start:
                    top[g, :, cols] = peak
                    total[g, :, cols] = jnp.sum(jnp.exp2(scores - peak), axis=0, keepdims=True)
                else:
                    old = top[g, :, cols]
                    new = jnp.maximum(old, peak)
                    top[g, :, cols] = new
                    total[g, :, cols] = total[g, :, cols] * jnp.exp2(old - new) + jnp.sum(
                        jnp.exp2(scores - new), axis=0, keepdims=True)
            return carry

        lax.fori_loop(0, kv_heads, head, 0)

    forward(n, True)
    forward(0)
    for step in range(1, half + 1):
        pass_on(0, step)
        if step < half:
            pass_on(1, step)
        forward(step)
        if step < half:
            forward(n - step)

    for g in range(kv_heads):
        top[g] = top[g] + jnp.log2(total[g])

    def value_side(spot, count):
        def head(g, carry):
            for b in range(count):
                span = slice((spot + b) * rows, (spot + b + 1) * rows)
                for c in range(chunks):
                    cols = slice(c * COLS, (c + 1) * COLS)
                    weights = jnp.exp2(st[g, span, cols] - top[g, :, cols])
                    st[g, span, cols] = weights
                    pb[b * rows:(b + 1) * rows, cols] = weights.astype(jnp.bfloat16)
            part[1, g, spot * rows:(spot + count) * rows, :] = dot(
                pb[0:count * rows, :], do_all[g])
            return carry

        lax.fori_loop(0, kv_heads, head, 0)

    def key_side(spot, count):
        def head(g, carry):
            for b in range(count):
                span = slice((spot + b) * rows, (spot + b + 1) * rows)
                values = vbuf[g, spot + b]
                for c in range(chunks):
                    cols = slice(c * COLS, (c + 1) * COLS)
                    moved = dot_nt(values, do_all[g, cols, :])
                    ds[g, span, cols] = (
                        st[g, span, cols] * (moved - delta[g, :, cols]) * scale
                    ).astype(jnp.bfloat16)
            part[0, g, spot * rows:(spot + count) * rows, :] = dot(
                ds[g, spot * rows:(spot + count) * rows, :], q_all[g])
            return carry

        lax.fori_loop(0, kv_heads, head, 0)

    def own(kind, g, spot):
        return part[kind, g, spot * rows:(spot + 1) * rows, :]

    def back_copy(kind, way, step, g):
        return send(
            snd.at[kind, way, step - 1, g], rcv.at[kind, way, step - 1, g],
            rs_send.at[kind, way, step - 1, g], rs_recv.at[kind, way, step - 1, g], way)

    back = {
        (kind, way, step, g): back_copy(kind, way, step, g)
        for kind in range(2) for way in range(2) for step in range(1, half + 1)
        for g in range(kv_heads) if step > 1 or g == way
    }

    value_side(order[half], 1)
    for way in range(2):
        snd[1, way, 0, way] = own(1, way, order[half]).astype(jnp.bfloat16)
        back[1, way, 1, way].start()
    pass_on(1, half)
    key_side(order[half], 1)
    for way in range(2):
        snd[0, way, 0, way] = own(0, way, order[half]).astype(jnp.bfloat16)
        back[0, way, 1, way].start()

    for step in range(2, half + 1):
        spot = 2 * (step - 2)
        for kind in (1, 0):
            if kind == 1:
                value_side(spot, 2)
            else:
                key_side(spot, 2)
            pairs = [(g, way) for g in range(kv_heads) for way in range(2)]
            if step == 2:
                pairs.sort(key=lambda pair: pair[0] == pair[1])
            for g, way in pairs:
                mine = own(kind, g, spot + way)
                if (kind, way, step - 1, g) in back:
                    back[kind, way, step - 1, g].wait_recv()
                    mine = mine + rcv[kind, way, step - 2, g].astype(jnp.float32)
                snd[kind, way, step - 1, g] = mine.astype(jnp.bfloat16)
                back[kind, way, step, g].start()

    spot = 2 * (half - 1)
    value_side(spot, 2)
    key_side(spot, 2)
    for kind in range(2):
        for g in range(kv_heads):
            drkv[kind, :, g * HD:(g + 1) * HD] = own(kind, g, spot + 1).astype(jnp.bfloat16)
    for g in range(kv_heads):
        for c in range(chunks):
            turned = dot(k_t[g], ds[g, :, c * COLS:(c + 1) * COLS])
            for j in range(COLS // rows):
                column = (g * ratio + c * (COLS // rows) + j) * HD
                q_in[:, column:column + HD] = jnp.transpose(
                    turned[:, j * rows:(j + 1) * rows]).astype(jnp.bfloat16)
    out_copies = [
        pltpu.make_async_copy(q_in, dq_ref, out_sem.at[0]),
        pltpu.make_async_copy(drkv, drkv_ref, out_sem.at[1]),
        pltpu.make_async_copy(dpkv, dpkv_ref, out_sem.at[2]),
    ]
    out_copies[0].start()
    out_copies[1].start()
    for kind in (1, 0):
        for g in range(kv_heads):
            summed = own(kind, g, spot)
            for way in range(2):
                back[kind, way, half, g].wait_recv()
                summed = summed + rcv[kind, way, half - 1, g].astype(jnp.float32)
            dpkv[kind, :, g * HD:(g + 1) * HD] = summed.astype(jnp.bfloat16)
    out_copies[2].start()

    for copy in list(gather.values()) + list(back.values()):
        copy.wait_send()
    for copy in out_copies:
        copy.wait()


def hand_out(a, b, c, a_out, b_out, c_out, a_held, b_held, c_held, in_sem, out_sem):
    triples = [(b, b_held, b_out), (c, c_held, c_out)]
    quarter = a.shape[0] // 4
    for i in range(4):
        span = pl.ds(i * quarter, quarter)
        triples.append((a.at[span], a_held.at[span], a_out.at[span]))
    taken = [pltpu.make_async_copy(t[0], t[1], in_sem.at[i]) for i, t in enumerate(triples)]
    given = [pltpu.make_async_copy(t[1], t[2], out_sem.at[i]) for i, t in enumerate(triples)]
    for copy in taken:
        copy.start()
    for copy, after in zip(taken, given):
        copy.wait()
        after.start()
    for copy in given:
        copy.wait()


def on_device(query, saved_out, d_out, resp_kv, prompt_kv, prefix_blocks, resp_len, block_position):
    rows = query.shape[0]
    kv_heads = resp_kv.shape[2] // HD
    ratio = query.shape[1] // HD // kv_heads
    axis_total = lax.axis_size("resp")
    n = min(16, axis_total)
    stride = axis_total // n
    half = n // 2
    wide = ratio * rows
    keys = (n + 1) * rows
    low, full = jnp.bfloat16, jnp.float32
    anywhere = pl.BlockSpec(memory_space=pl.ANY)
    smem = pl.BlockSpec(memory_space=pltpu.SMEM)
    dma = pltpu.SemaphoreType.DMA
    results = pl.pallas_call(
        functools.partial(kernel, n, stride, kv_heads, ratio, rows),
        out_shape=(
            jax.ShapeDtypeStruct(query.shape, low),
            jax.ShapeDtypeStruct(resp_kv.shape, low),
            jax.ShapeDtypeStruct(prompt_kv.shape, low),
        ),
        in_specs=[anywhere] * 5 + [smem] * 3,
        out_specs=(anywhere, anywhere, anywhere),
        scratch_shapes=[
            pltpu.VMEM(query.shape, low),
            pltpu.VMEM(query.shape, low),
            pltpu.VMEM(query.shape, low),
            pltpu.VMEM((kv_heads, wide, HD), low),
            pltpu.VMEM((kv_heads, wide, HD), low),
            pltpu.VMEM((kv_heads, n + 1, rows + POS_ROWS, HD), low),
            pltpu.VMEM((kv_heads, n + 1, rows, HD), low),
            pltpu.VMEM((kv_heads, HD, keys), low),
            pltpu.VMEM((kv_heads, 1, wide), full),
            pltpu.VMEM((kv_heads, 1, wide), full),
            pltpu.VMEM((kv_heads, 1, wide), full),
            pltpu.VMEM((kv_heads, keys, wide), full),
            pltpu.VMEM((2 * rows, wide), low),
            pltpu.VMEM((kv_heads, keys, wide), low),
            pltpu.VMEM((2, kv_heads, keys, HD), full),
            pltpu.VMEM((2, 2, half, kv_heads, rows, HD), low),
            pltpu.VMEM((2, 2, half, kv_heads, rows, HD), low),
            pltpu.VMEM(resp_kv.shape, low),
            pltpu.VMEM(prompt_kv.shape, low),
            dma((3,)),
            dma((3,)),
            dma((4, kv_heads)),
            dma((2, 2, half, kv_heads)),
            dma((2, 2, half, kv_heads)),
            dma((2, 2, half, kv_heads)),
            dma((2, 2, half, kv_heads)),
        ],
        compiler_params=pltpu.CompilerParams(
            collective_id=0, has_side_effects=True, vmem_limit_bytes=56 * 2**20),
    )(query, saved_out, d_out, resp_kv, prompt_kv, prefix_blocks, resp_len, block_position)
    return pl.pallas_call(
        hand_out,
        out_shape=tuple(jax.ShapeDtypeStruct(r.shape, r.dtype) for r in results),
        in_specs=[anywhere] * 3,
        out_specs=(anywhere,) * 3,
        scratch_shapes=[pltpu.VMEM(r.shape, r.dtype) for r in results] + [dma((6,)), dma((6,))],
    )(*results)


def solution(mesh):
    placed = (
        P(("groups", "resp"), "mp"),
        P(("groups", "resp"), "mp"),
        P(("groups", "resp"), "mp"),
        P(None, ("groups", "resp"), "mp"),
        P(None, ("groups", "resp"), "mp"),
        P(("groups", "resp")),
        P(("groups", "resp")),
        P(("groups", "resp")),
    )
    return jax.shard_map(
        on_device,
        mesh=mesh,
        in_specs=placed,
        out_specs=(
            P(("groups", "resp"), "mp"),
            P(None, ("groups", "resp"), "mp"),
            P(None, ("groups", "resp"), "mp"),
        ),
        check_vma=False,
    )
```
